512 devices in a mesh: sect: 8 (over y_hi, x), slab: 32 (over z, y_lo), energy: 2 (over core).
Axes of the slice: x: 4, y: 4 (y_hi: 2, y_lo: 2; y = y_hi * 2 + y_lo), z: 16, core: 2. Of those that a mesh axis runs over, the one named last changes fastest.
Arguments:
- source: bfloat16 [16, 2048, 128], P(('energy', 'sect'), 'slab'), parts along dimension 0, may hold values from -6 to 6
- forward_mult: bfloat16 [16, 2, 2048, 2048], P(('energy', 'sect'), None, 'slab'), parts along dimension 0, may hold values from -0.09375 to 0.09375
- schur_inverse: bfloat16 [16, 2, 2048, 2048], P(('energy', 'sect'), None, 'slab'), parts along dimension 0, may hold values from -0.046875 to 0.046875
- upper_mult: bfloat16 [16, 2, 2048, 2048], P(('energy', 'sect'), None, 'slab'), parts along dimension 0, may hold values from -0.0625 to 0.0625
Outputs:
- wave: bfloat16 [16, 2048, 128], P(('energy', 'sect'), 'slab'), parts along dimension 0
The draws below stay inside these ranges and needn't reach their ends.
There are 2 independent parts, one for each index of `energy`. The reference program is written for one: setup_inputs(seed, part) draws one part's arguments, and reference() takes and returns one part's arrays. A program takes and returns all parts, laid end to end along the dimension named above; each array names one. Nothing has to cross between parts.
All inputs are finite; a program needn't handle non-finite values.
Results may differ from the reference program's by a relative error of at most 0.012.
Values may be sent and summed in bfloat16 or wider, within the bound.
A program may use at most 64 MiB of HBM per device.

```python
import jax
import jax.numpy as jnp

MODES = 64
ORDER = 2048
SECTIONS = 8


def shard_levels(key, dims, pieces, least, high):
    def one(position, shards_of):
        steps = jax.random.uniform(jax.random.fold_in(jax.random.fold_in(key, 6), position), (shards_of,), jnp.float32, least / len(pieces), high / len(pieces))
        return jnp.repeat(jnp.exp(steps), dims[position] // shards_of).reshape((-1,) + (1,) * (len(dims) - position - 1))

    factor_of = one(*pieces[0])
    for cut in pieces[1:]:
        factor_of = factor_of * one(*cut)
    return factor_of


def noise(stream_key, dims, scale, reach, pieces=(), held_as=jnp.bfloat16):
    drawn = scale * jax.random.normal(stream_key, dims, jnp.float32)
    if pieces:
        drawn = drawn * shard_levels(stream_key, dims, pieces, -0.22, 0.18)
    return jnp.clip(drawn, -reach, reach).astype(held_as)


def setup_inputs(seed: int = 0, part: int = 0) -> dict:
    key_of = jax.random.split(jax.random.key(seed), 5)
    own_keys = jax.random.split(jax.random.fold_in(key_of[4], part), 5)
    source = noise(own_keys[0], (SECTIONS, ORDER, 2 * MODES), 1.0, 6.0, ((0, 8), (1, 32)))
    forward_mult = noise(own_keys[1], (SECTIONS, 2, ORDER, ORDER), (2 * ORDER) ** -0.5, 0.09375, ((0, 8), (2, 32)))
    schur_inverse = noise(own_keys[2], (SECTIONS, 2, ORDER, ORDER), (8 * ORDER) ** -0.5, 0.046875, ((0, 8), (2, 32)))
    upper_mult = noise(own_keys[3], (SECTIONS, 2, ORDER, ORDER), (4 * ORDER) ** -0.5, 0.0625, ((0, 8), (2, 32)))
    return {"source": source, "forward_mult": forward_mult, "schur_inverse": schur_inverse, "upper_mult": upper_mult}


def complex_apply(matrix, vector):
    half_cols = vector.shape[1] // 2
    real_part = jnp.dot(matrix[0], vector, preferred_element_type=jnp.float32)
    imag_part = jnp.dot(matrix[1], vector, preferred_element_type=jnp.float32)
    return jnp.concatenate([real_part[:, :half_cols] - imag_part[:, half_cols:], real_part[:, half_cols:] + imag_part[:, :half_cols]], axis=1)


def reference(source, forward_mult, schur_inverse, upper_mult):
    sections = source.shape[0]
    previous = jnp.zeros_like(source[0])
    forward_list = []
    for section in range(sections):
        previous = (source[section].astype(jnp.float32) + complex_apply(forward_mult[section], previous)).astype(jnp.bfloat16)
        forward_list.append(previous)
    following = jnp.zeros_like(source[0])
    waves = [following] * sections
    for section in reversed(range(sections)):
        scaled = complex_apply(schur_inverse[section], forward_list[section])
        following = (scaled - complex_apply(upper_mult[section], following)).astype(jnp.bfloat16)
        waves[section] = following
    return jnp.stack(waves)
```

```python
import functools

import jax
import jax.numpy as jnp
from jax import lax
from jax.experimental import pallas as pl
from jax.experimental.pallas import tpu as pltpu
from jax.sharding import PartitionSpec as P

MESH = pl.DeviceIdType.MESH
CHUNKS = 4


def kernel(sections, slabs, src_hbm, fwd_hbm, inv_hbm, upp_hbm, out_ref,
           src_v, mats, weights, src_t, scaled, f_tile, w_tile,
           f_all, s_all, w_all, load_sem, send_sem, f_sem, s_sem, w_sem, back_sem):
    sect = lax.axis_index("sect")
    slab = lax.axis_index("slab")
    planes = slabs // 2
    z, y = slab // 2, lax.rem(slab, 2)
    rows = src_v.shape[0]
    modes = src_v.shape[1] // 2
    width = modes // CHUNKS

    def member(t):
        i, dy = t // 2, lax.rem(t, 2)
        reach = planes // 2 - (i + 1) // 2
        dz = jnp.where(lax.rem(i, 2) == 0, -reach, reach)
        zz = lax.rem(z + dz + planes, planes)
        yy = lax.rem(y + 1 + dy, 2)
        return zz * 2 + yy

    barrier = pltpu.get_barrier_semaphore()

    @pl.when(sect > 0)
    def _():
        def greet(t, _):
            pl.semaphore_signal(barrier, inc=1, device_id={"sect": sect - 1, "slab": member(t)}, device_id_type=MESH)
            return 0
        lax.fori_loop(0, slabs, greet, 0)

    loads = [pltpu.make_async_copy(src_hbm.at[0], src_v, load_sem.at[3])]
    loads += [
        pltpu.make_async_copy(ref.at[0], mats.at[i], load_sem.at[i])
        for i, ref in enumerate((fwd_hbm, inv_hbm, upp_hbm))
    ]
    for load in loads:
        load.start()

    def send_all(tile, gathered, sem, c, to_sect, skip_self):
        def one(t, _):
            to = member(t)
            pltpu.make_async_remote_copy(
                src_ref=tile.at[c], dst_ref=gathered.at[c, slab],
                send_sem=send_sem.at[c], recv_sem=sem.at[c],
                device_id={"sect": to_sect, "slab": to}, device_id_type=MESH,
            ).start()
            return 0
        lax.fori_loop(0, slabs - 1 if skip_self else slabs, one, 0)

    def wait_for(gathered, sem, c, count):
        part = gathered.at[c, pl.ds(0, count)]
        pltpu.make_async_copy(part, part, sem.at[c]).wait()

    loads[0].wait()
    both = src_v[...].astype(jnp.float32)
    turned = jnp.concatenate([both[:, :modes], both[:, modes:]], axis=0).T
    for c in range(CHUNKS):
        src_t[c] = turned[c * width:(c + 1) * width]

    @pl.when(sect < sections - 1)
    def _():
        pl.semaphore_wait(barrier, slabs)

    @pl.when(sect == 0)
    def _():
        for c in range(CHUNKS):
            f_tile[c] = src_t[c].astype(jnp.bfloat16)
            send_all(f_tile, f_all, f_sem, c, 1, False)

    def prepare(i):
        loads[1 + i].wait()

        def pair(j, _):
            at = pl.ds(pl.multiple_of(j * 2 * rows, 2 * rows), 2 * rows)
            p0 = mats[i, 0, :, at]
            p1 = mats[i, 1, :, at]
            lo0, hi0 = p0[:, :rows], p0[:, rows:]
            lo1, hi1 = p1[:, :rows], p1[:, rows:]
            out_at = pl.ds(pl.multiple_of(j * 4 * rows, 4 * rows), 4 * rows)
            weights[i, pl.ds(0, rows), out_at] = jnp.concatenate([lo0, -lo1, hi0, -hi1], axis=1)
            weights[i, pl.ds(rows, rows), out_at] = jnp.concatenate([lo1, lo0, hi1, hi0], axis=1)
            return 0

        lax.fori_loop(0, slabs // 2, pair, 0)

    def apply(i, gathered, c):
        lhs = jnp.concatenate([gathered[c, k] for k in range(slabs)], axis=1)
        return lax.dot_general(
            lhs, weights[i], (((1,), (1,)), ((), ())), preferred_element_type=jnp.float32
        )

    for i in range(3):
        prepare(i)

    @pl.when(sect > 0)
    def _():
        for c in range(CHUNKS):
            wait_for(f_all, f_sem, c, slabs)
            pltpu.make_async_remote_copy(
                src_ref=f_all.at[c], dst_ref=s_all.at[c],
                send_sem=back_sem.at[c], recv_sem=s_sem.at[c],
                device_id={"sect": sect - 1}, device_id_type=MESH,
            ).start()
            f_tile[c] = (src_t[c] + apply(0, f_all, c)).astype(jnp.bfloat16)

            @pl.when(sect < sections - 1)
            def _():
                send_all(f_tile, f_all, f_sem, c, sect + 1, False)

            @pl.when(sect == sections - 1)
            def _():
                s_all[c, slab] = f_tile[c]
                send_all(f_tile, s_all, s_sem, c, sect, True)

    for c in range(CHUNKS):
        @pl.when(sect < sections - 1)
        def _():
            wait_for(s_all, s_sem, c, slabs)

        @pl.when(sect == sections - 1)
        def _():
            wait_for(s_all, s_sem, c, slabs - 1)
        scaled[c] = apply(1, s_all, c)

        @pl.when(sect == sections - 1)
        def _():
            wait_for(s_all, send_sem, c, slabs - 1)
            w_tile[c] = scaled[c].astype(jnp.bfloat16)
            send_all(w_tile, w_all, w_sem, c, sect - 1, False)

    @pl.when(sect < sections - 1)
    def _():
        for c in range(CHUNKS):
            wait_for(w_all, w_sem, c, slabs)
            wait_for(f_all, send_sem, c, slabs)
            w_tile[c] = (scaled[c] - apply(2, w_all, c)).astype(jnp.bfloat16)

            @pl.when(sect > 0)
            def _():
                send_all(w_tile, w_all, w_sem, c, sect - 1, False)

    wave = jnp.concatenate([w_tile[c] for c in range(CHUNKS)], axis=0).astype(jnp.float32).T
    out_ref[0] = jnp.concatenate([wave[:rows], wave[rows:]], axis=1).astype(jnp.bfloat16)

    @pl.when(sect > 0)
    def _():
        for c in range(CHUNKS):
            wait_for(w_all, send_sem, c, slabs)
            wait_for(f_all, back_sem, c, slabs)


def per_device(source, forward_mult, schur_inverse, upper_mult):
    sections = lax.axis_size("sect")
    slabs = lax.axis_size("slab")
    _, rows, columns = source.shape
    width = columns // 2 // CHUNKS
    gathered = pltpu.VMEM((CHUNKS, slabs, width, 2 * rows), jnp.bfloat16)
    tile = pltpu.VMEM((CHUNKS, width, 2 * rows), jnp.bfloat16)
    tile32 = pltpu.VMEM((CHUNKS, width, 2 * rows), jnp.float32)
    return pl.pallas_call(
        functools.partial(kernel, sections, slabs),
        out_shape=jax.ShapeDtypeStruct(source.shape, source.dtype),
        in_specs=[pl.BlockSpec(memory_space=pl.ANY)] * 4,
        out_specs=pl.BlockSpec(memory_space=pltpu.VMEM),
        scratch_shapes=[
            pltpu.VMEM((rows, columns), jnp.bfloat16),
            pltpu.VMEM((3, 2, rows, slabs * rows), jnp.bfloat16),
            pltpu.VMEM((3, 2 * rows, slabs * 2 * rows), jnp.bfloat16),
            tile32,
            tile32,
            tile,
            tile,
            gathered,
            gathered,
            gathered,
            pltpu.SemaphoreType.DMA((4,)),
            pltpu.SemaphoreType.DMA((CHUNKS,)),
            pltpu.SemaphoreType.DMA((CHUNKS,)),
            pltpu.SemaphoreType.DMA((CHUNKS,)),
            pltpu.SemaphoreType.DMA((CHUNKS,)),
            pltpu.SemaphoreType.DMA((CHUNKS,)),
        ],
        compiler_params=pltpu.CompilerParams(
            collective_id=0, has_side_effects=True, vmem_limit_bytes=40 * 1024 * 1024
        ),
    )(source, forward_mult, schur_inverse, upper_mult)


def solution(mesh):
    in_specs = (
        P(("energy", "sect"), "slab", None),
        P(("energy", "sect"), None, "slab", None),
        P(("energy", "sect"), None, "slab", None),
        P(("energy", "sect"), None, "slab", None),
    )
    out_specs = P(("energy", "sect"), "slab", None)
    return jax.shard_map(
        per_device, mesh=mesh, in_specs=in_specs, out_specs=out_specs, check_vma=False
    )
```

```python
import functools

import jax
import jax.numpy as jnp
from jax import lax
from jax.experimental import pallas as pl
from jax.experimental.pallas import tpu as pltpu
from jax.sharding import PartitionSpec as P

MESH = pl.DeviceIdType.MESH
CHUNKS = 8


def kernel(sections, slabs, src_hbm, fwd_hbm, inv_hbm, upp_hbm, out_ref,
           src_v, mats, weights, src_t, scaled, f_tile, w_tile,
           f_all, s_all, w_all, load_sem, send_sem, f_sem, s_sem, w_sem, back_sem):
    sect = lax.axis_index("sect")
    slab = lax.axis_index("slab")
    planes = slabs // 2
    z, y = slab // 2, lax.rem(slab, 2)
    rows = src_v.shape[0]
    modes = src_v.shape[1] // 2
    width = modes // CHUNKS

    def member(t):
        i, dy = t // 2, lax.rem(t, 2)
        reach = planes // 2 - (i + 1) // 2
        dz = jnp.where(lax.rem(i, 2) == 0, -reach, reach)
        zz = lax.rem(z + dz + planes, planes)
        yy = lax.rem(y + 1 + dy, 2)
        return zz * 2 + yy

    barrier = pltpu.get_barrier_semaphore()

    @pl.when(sect > 0)
    def _():
        def greet(t, _):
            pl.semaphore_signal(barrier, inc=1, device_id={"sect": sect - 1, "slab": member(t)}, device_id_type=MESH)
            return 0
        lax.fori_loop(0, slabs, greet, 0)

    loads = [pltpu.make_async_copy(src_hbm.at[0], src_v, load_sem.at[3])]
    loads += [
        pltpu.make_async_copy(ref.at[0], mats.at[i], load_sem.at[i])
        for i, ref in enumerate((fwd_hbm, inv_hbm, upp_hbm))
    ]
    for load in loads:
        load.start()

    def send_all(tile, gathered, sem, c, to_sect, skip_self):
        def one(t, _):
            to = member(t)
            pltpu.make_async_remote_copy(
                src_ref=tile.at[c], dst_ref=gathered.at[c, slab],
                send_sem=send_sem.at[c], recv_sem=sem.at[c],
                device_id={"sect": to_sect, "slab": to}, device_id_type=MESH,
            ).start()
            return 0
        lax.fori_loop(0, slabs - 1 if skip_self else slabs, one, 0)

    def wait_for(gathered, sem, c, count):
        part = gathered.at[c, pl.ds(0, count)]
        pltpu.make_async_copy(part, part, sem.at[c]).wait()

    loads[0].wait()
    both = src_v[...].astype(jnp.float32)
    turned = jnp.concatenate([both[:, :modes], both[:, modes:]], axis=0).T
    for c in range(CHUNKS):
        src_t[c] = turned[c * width:(c + 1) * width]

    @pl.when(sect < sections - 1)
    def _():
        pl.semaphore_wait(barrier, slabs)

    @pl.when(sect == 0)
    def _():
        for c in range(CHUNKS):
            f_tile[c] = src_t[c].astype(jnp.bfloat16)
            send_all(f_tile, f_all, f_sem, c, 1, False)

    def prepare(i):
        loads[1 + i].wait()

        def pair(j, _):
            at = pl.ds(pl.multiple_of(j * 2 * rows, 2 * rows), 2 * rows)
            p0 = mats[i, 0, :, at]
            p1 = mats[i, 1, :, at]
            lo0, hi0 = p0[:, :rows], p0[:, rows:]
            lo1, hi1 = p1[:, :rows], p1[:, rows:]
            out_at = pl.ds(pl.multiple_of(j * 4 * rows, 4 * rows), 4 * rows)
            weights[i, pl.ds(0, rows), out_at] = jnp.concatenate([lo0, -lo1, hi0, -hi1], axis=1)
            weights[i, pl.ds(rows, rows), out_at] = jnp.concatenate([lo1, lo0, hi1, hi0], axis=1)
            return 0

        lax.fori_loop(0, slabs // 2, pair, 0)

    def apply(i, gathered, c):
        lhs = jnp.concatenate([gathered[c, k] for k in range(slabs)], axis=1)
        return lax.dot_general(
            lhs, weights[i], (((1,), (1,)), ((), ())), preferred_element_type=jnp.float32
        )

    for i in range(3):
        prepare(i)

    @pl.when(sect > 0)
    def _():
        for c in range(CHUNKS):
            wait_for(f_all, f_sem, c, slabs)
            pltpu.make_async_remote_copy(
                src_ref=f_all.at[c], dst_ref=s_all.at[c],
                send_sem=back_sem.at[c], recv_sem=s_sem.at[c],
                device_id={"sect": sect - 1}, device_id_type=MESH,
            ).start()
            f_tile[c] = (src_t[c] + apply(0, f_all, c)).astype(jnp.bfloat16)

            @pl.when(sect < sections - 1)
            def _():
                send_all(f_tile, f_all, f_sem, c, sect + 1, False)

            @pl.when(sect == sections - 1)
            def _():
                s_all[c, slab] = f_tile[c]
                send_all(f_tile, s_all, s_sem, c, sect, True)

    for c in range(CHUNKS):
        @pl.when(sect < sections - 1)
        def _():
            wait_for(s_all, s_sem, c, slabs)

        @pl.when(sect == sections - 1)
        def _():
            wait_for(s_all, s_sem, c, slabs - 1)
        scaled[c] = apply(1, s_all, c)

        @pl.when(sect == sections - 1)
        def _():
            wait_for(s_all, send_sem, c, slabs - 1)
            w_tile[c] = scaled[c].astype(jnp.bfloat16)
            send_all(w_tile, w_all, w_sem, c, sect - 1, False)

    @pl.when(sect < sections - 1)
    def _():
        for c in range(CHUNKS):
            wait_for(w_all, w_sem, c, slabs)
            wait_for(f_all, send_sem, c, slabs)
            w_tile[c] = (scaled[c] - apply(2, w_all, c)).astype(jnp.bfloat16)

            @pl.when(sect > 0)
            def _():
                send_all(w_tile, w_all, w_sem, c, sect - 1, False)

    wave = jnp.concatenate([w_tile[c] for c in range(CHUNKS)], axis=0).astype(jnp.float32).T
    out_ref[0] = jnp.concatenate([wave[:rows], wave[rows:]], axis=1).astype(jnp.bfloat16)

    @pl.when(sect > 0)
    def _():
        for c in range(CHUNKS):
            wait_for(w_all, send_sem, c, slabs)
            wait_for(f_all, back_sem, c, slabs)


def per_device(source, forward_mult, schur_inverse, upper_mult):
    sections = lax.axis_size("sect")
    slabs = lax.axis_size("slab")
    _, rows, columns = source.shape
    width = columns // 2 // CHUNKS
    gathered = pltpu.VMEM((CHUNKS, slabs, width, 2 * rows), jnp.bfloat16)
    tile = pltpu.VMEM((CHUNKS, width, 2 * rows), jnp.bfloat16)
    tile32 = pltpu.VMEM((CHUNKS, width, 2 * rows), jnp.float32)
    return pl.pallas_call(
        functools.partial(kernel, sections, slabs),
        out_shape=jax.ShapeDtypeStruct(source.shape, source.dtype),
        in_specs=[pl.BlockSpec(memory_space=pl.ANY)] * 4,
        out_specs=pl.BlockSpec(memory_space=pltpu.VMEM),
        scratch_shapes=[
            pltpu.VMEM((rows, columns), jnp.bfloat16),
            pltpu.VMEM((3, 2, rows, slabs * rows), jnp.bfloat16),
            pltpu.VMEM((3, 2 * rows, slabs * 2 * rows), jnp.bfloat16),
            tile32,
            tile32,
            tile,
            tile,
            gathered,
            gathered,
            gathered,
            pltpu.SemaphoreType.DMA((4,)),
            pltpu.SemaphoreType.DMA((CHUNKS,)),
            pltpu.SemaphoreType.DMA((CHUNKS,)),
            pltpu.SemaphoreType.DMA((CHUNKS,)),
            pltpu.SemaphoreType.DMA((CHUNKS,)),
            pltpu.SemaphoreType.DMA((CHUNKS,)),
        ],
        compiler_params=pltpu.CompilerParams(
            collective_id=0, has_side_effects=True, vmem_limit_bytes=40 * 1024 * 1024
        ),
    )(source, forward_mult, schur_inverse, upper_mult)


def solution(mesh):
    in_specs = (
        P(("energy", "sect"), "slab", None),
        P(("energy", "sect"), None, "slab", None),
        P(("energy", "sect"), None, "slab", None),
        P(("energy", "sect"), None, "slab", None),
    )
    out_specs = P(("energy", "sect"), "slab", None)
    return jax.shard_map(
        per_device, mesh=mesh, in_specs=in_specs, out_specs=out_specs, check_vma=False
    )
```

```python
import functools

import jax
import jax.numpy as jnp
from jax import lax
from jax.experimental import pallas as pl
from jax.experimental.pallas import tpu as pltpu
from jax.sharding import PartitionSpec as P

MESH = pl.DeviceIdType.MESH
CHUNKS = 8
BACK_LAG = 5


def kernel(sections, slabs, src_hbm, fwd_hbm, inv_hbm, upp_hbm, out_ref,
           src_v, mats, weights, src_t, scaled, f_tile, w_tile,
           t_tile, f_all, s_all, w_all, t_all, load_sem, f_sent, w_sent, t_sent,
           f_sem, s_sem, w_sem, t_sem, back_sem, lend_sem, home_sem):
    sect = lax.axis_index("sect")
    slab = lax.axis_index("slab")
    planes = slabs // 2
    z, y = slab // 2, lax.rem(slab, 2)
    last = sections - 1
    helper = sections - 4
    rows = src_v.shape[0]
    modes = src_v.shape[1] // 2
    width = modes // CHUNKS

    members = []
    for i in range(planes):
        reach = planes // 2 - (i + 1) // 2
        zz = lax.rem(z + (reach if i % 2 else planes - reach), planes)
        members += [zz * 2 + 1 - y, zz * 2 + y]

    barrier = pltpu.get_barrier_semaphore()

    @pl.when(sect > 0)
    def _():
        for to in members:
            pl.semaphore_signal(barrier, inc=1, device_id={"sect": sect - 1, "slab": to}, device_id_type=MESH)

    @pl.when(sect == helper)
    def _():
        pl.semaphore_signal(barrier, inc=1, device_id={"sect": last}, device_id_type=MESH)

    loads = [pltpu.make_async_copy(src_hbm.at[0], src_v, load_sem.at[3])]
    loads += [
        pltpu.make_async_copy(ref.at[0], mats.at[i], load_sem.at[i])
        for i, ref in enumerate((fwd_hbm, inv_hbm, upp_hbm))
    ]
    for load in loads:
        load.start()

    def send_all(tile, gathered, sent, sem, c, to_sect):
        for to in members:
            pltpu.make_async_remote_copy(
                src_ref=tile.at[c], dst_ref=gathered.at[c, slab],
                send_sem=sent.at[c], recv_sem=sem.at[c],
                device_id={"sect": to_sect, "slab": to}, device_id_type=MESH,
            ).start()

    def wait_for(gathered, sem, c):
        pltpu.make_async_copy(gathered.at[c], gathered.at[c], sem.at[c]).wait()

    loads[0].wait()
    both = src_v[...].astype(jnp.float32)
    turned = jnp.concatenate([both[:, :modes], both[:, modes:]], axis=0).T
    for c in range(CHUNKS):
        src_t[c] = turned[c * width:(c + 1) * width]

    lend = pltpu.make_async_remote_copy(
        src_ref=inv_hbm.at[0], dst_ref=mats.at[3],
        send_sem=lend_sem.at[0], recv_sem=lend_sem.at[1],
        device_id={"sect": helper}, device_id_type=MESH,
    )

    @pl.when(sect < last)
    def _():
        pl.semaphore_wait(barrier, slabs)

    @pl.when(sect == last)
    def _():
        pl.semaphore_wait(barrier, 1)
        lend.start()

    def each_chunk(body):
        def step(c, _):
            body(c)
            return 0
        lax.fori_loop(0, CHUNKS, step, 0)

    @pl.when(sect == 0)
    def _():
        def first(c):
            f_tile[c] = src_t[c].astype(jnp.bfloat16)
            send_all(f_tile, f_all, f_sent, f_sem, c, 1)

        each_chunk(first)

    def prepare(i):
        if i < 3:
            loads[1 + i].wait()
        else:
            pltpu.make_async_copy(mats.at[3], mats.at[3], lend_sem.at[1]).wait()

        def pair(j, _):
            at = pl.ds(pl.multiple_of(j * 2 * rows, 2 * rows), 2 * rows)
            p0 = mats[i, 0, :, at].astype(jnp.float32).T.astype(jnp.bfloat16)
            p1 = mats[i, 1, :, at].astype(jnp.float32).T.astype(jnp.bfloat16)
            blocks = []
            for k in range(2):
                q0, q1 = p0[k * rows:(k + 1) * rows], p1[k * rows:(k + 1) * rows]
                blocks.append(jnp.concatenate([q0, q1], axis=1))
                blocks.append(jnp.concatenate([-q1, q0], axis=1))
            weights[i, pl.ds(pl.multiple_of(j * 4 * rows, 4 * rows), 4 * rows)] = jnp.concatenate(blocks, axis=0)
            return 0

        lax.fori_loop(0, slabs // 2, pair, 0)

    def apply(i, gathered, c):
        lhs = jnp.concatenate([gathered[c, k] for k in range(slabs)], axis=1)
        return jnp.dot(lhs, weights[i], preferred_element_type=jnp.float32)

    prepare(0)

    @pl.when(sect > 1)
    def _():
        prepare(1)
        prepare(2)

    def forward(c):
        wait_for(f_all, f_sem, c)
        f_tile[c] = (src_t[c] + apply(0, f_all, c)).astype(jnp.bfloat16)

        @pl.when(sect < last)
        def _():
            send_all(f_tile, f_all, f_sent, f_sem, c, sect + 1)

        @pl.when(sect == last)
        def _():
            send_all(f_tile, t_all, f_sent, t_sem, c, helper)

        pltpu.make_async_remote_copy(
            src_ref=f_all.at[c], dst_ref=s_all.at[c],
            send_sem=back_sem.at[c], recv_sem=s_sem.at[c],
            device_id={"sect": sect - 1}, device_id_type=MESH,
        ).start()

    def turn(c):
        wait_for(t_all, t_sem, c)
        t_tile[c] = apply(3, t_all, c).astype(jnp.bfloat16)
        send_all(t_tile, w_all, t_sent, w_sem, c, last - 1)

    def scale(c):
        wait_for(s_all, s_sem, c)
        scaled[c] = apply(1, s_all, c)

    def backward(c):
        wait_for(w_all, w_sem, c)
        w_tile[c] = (scaled[c] - apply(2, w_all, c)).astype(jnp.bfloat16)

        @pl.when(sect > 0)
        def _():
            send_all(w_tile, w_all, w_sent, w_sem, c, sect - 1)

    home = pltpu.make_async_remote_copy(
        src_ref=t_tile, dst_ref=w_tile,
        send_sem=home_sem.at[0], recv_sem=home_sem.at[1],
        device_id={"sect": last}, device_id_type=MESH,
    )

    @pl.when(sect > 0)
    def _():
        each_chunk(forward)

    @pl.when(sect <= 1)
    def _():
        prepare(1)
        prepare(2)

    @pl.when(sect < last - 1)
    def _():
        each_chunk(scale)

        @pl.when(sect == helper)
        def _():
            prepare(3)
            each_chunk(turn)
            home.start()

        each_chunk(backward)

    @pl.when(sect == last - 1)
    def _():
        def step(c, _):
            @pl.when(c < CHUNKS)
            def _():
                scale(c)

            @pl.when(c >= BACK_LAG)
            def _():
                backward(c - BACK_LAG)
            return 0
        lax.fori_loop(0, CHUNKS + BACK_LAG, step, 0)

    @pl.when(sect == last)
    def _():
        home.wait_recv()

    wave = jnp.concatenate([w_tile[c] for c in range(CHUNKS)], axis=0).astype(jnp.float32).T
    out_ref[0] = jnp.concatenate([wave[:rows], wave[rows:]], axis=1).astype(jnp.bfloat16)

    @each_chunk
    def _(c):
        wait_for(f_all, f_sent, c)

        @pl.when(sect > 0)
        def _():
            wait_for(f_all, back_sem, c)

        @pl.when((sect > 0) & (sect < last))
        def _():
            wait_for(w_all, w_sent, c)

        @pl.when(sect == helper)
        def _():
            wait_for(w_all, t_sent, c)

    @pl.when(sect == helper)
    def _():
        home.wait_send()

    @pl.when(sect == last)
    def _():
        lend.wait_send()


def per_device(source, forward_mult, schur_inverse, upper_mult):
    sections = lax.axis_size("sect")
    slabs = lax.axis_size("slab")
    _, rows, columns = source.shape
    width = columns // 2 // CHUNKS
    gathered = pltpu.VMEM((CHUNKS, slabs, width, 2 * rows), jnp.bfloat16)
    tile = pltpu.VMEM((CHUNKS, width, 2 * rows), jnp.bfloat16)
    tile32 = pltpu.VMEM((CHUNKS, width, 2 * rows), jnp.float32)
    return pl.pallas_call(
        functools.partial(kernel, sections, slabs),
        out_shape=jax.ShapeDtypeStruct(source.shape, source.dtype),
        in_specs=[pl.BlockSpec(memory_space=pltpu.HBM)] * 4,
        out_specs=pl.BlockSpec(memory_space=pltpu.VMEM),
        scratch_shapes=[
            pltpu.VMEM((rows, columns), jnp.bfloat16),
            pltpu.VMEM((4, 2, rows, slabs * rows), jnp.bfloat16),
            pltpu.VMEM((4, slabs * 2 * rows, 2 * rows), jnp.bfloat16),
            tile32,
            tile32,
            tile,
            tile,
            tile,
            gathered,
            gathered,
            gathered,
            gathered,
            pltpu.SemaphoreType.DMA((4,)),
            pltpu.SemaphoreType.DMA((CHUNKS,)),
            pltpu.SemaphoreType.DMA((CHUNKS,)),
            pltpu.SemaphoreType.DMA((CHUNKS,)),
            pltpu.SemaphoreType.DMA((CHUNKS,)),
            pltpu.SemaphoreType.DMA((CHUNKS,)),
            pltpu.SemaphoreType.DMA((CHUNKS,)),
            pltpu.SemaphoreType.DMA((CHUNKS,)),
            pltpu.SemaphoreType.DMA((CHUNKS,)),
            pltpu.SemaphoreType.DMA((2,)),
            pltpu.SemaphoreType.DMA((2,)),
        ],
        compiler_params=pltpu.CompilerParams(
            collective_id=0, has_side_effects=True, vmem_limit_bytes=40 * 1024 * 1024
        ),
    )(source, forward_mult, schur_inverse, upper_mult)


def solution(mesh):
    in_specs = (
        P(("energy", "sect"), "slab", None),
        P(("energy", "sect"), None, "slab", None),
        P(("energy", "sect"), None, "slab", None),
        P(("energy", "sect"), None, "slab", None),
    )
    out_specs = P(("energy", "sect"), "slab", None)
    return jax.shard_map(
        per_device, mesh=mesh, in_specs=in_specs, out_specs=out_specs, check_vma=False
    )
```

```python
import functools

import jax
import jax.numpy as jnp
from jax import lax
from jax.experimental import pallas as pl
from jax.experimental.pallas import tpu as pltpu
from jax.sharding import PartitionSpec as P

MESH = pl.DeviceIdType.MESH
CHUNKS = 8
OWN = 5


def kernel(sections, slabs, src_hbm, fwd_hbm, inv_hbm, upp_hbm, out_ref,
           src_v, mats, weights, src_t, scaled, f_tile, w_tile, t_tile, w_home,
           f_all, s_all, w_all, t_all, load_sem, f_sent, w_sent, t_sent,
           f_sem, s_sem, w_sem, t_sem, back_sem, lend_sent, lend_sem, home_sent, home_sem):
    sect = lax.axis_index("sect")
    slab = lax.axis_index("slab")
    planes = slabs // 2
    z, y = slab // 2, lax.rem(slab, 2)
    last = sections - 1
    half = sections // 2
    rows = src_v.shape[1]
    modes = src_v.shape[2] // 2
    width = modes // CHUNKS
    mirror = slab + 1 - 2 * y
    partner = {"sect": lax.rem(sect + half, sections), "slab": mirror}
    after = lax.rem(sect + 1, sections)
    before = lax.rem(sect + last, sections)
    upper = sect >= half
    low_pipe = jnp.where(upper, 1, 0)
    high_pipe = 1 - low_pipe
    low = lax.rem(sect, half)
    high = low + half
    firsts = (0, OWN)
    counts = (OWN, CHUNKS - OWN)

    members = []
    for i in range(planes):
        reach = planes // 2 - (i + 1) // 2
        zz = lax.rem(z + (reach if i % 2 else planes - reach), planes)
        members += [zz * 2 + 1 - y, zz * 2 + y]

    barrier = pltpu.get_barrier_semaphore()
    pl.semaphore_signal(barrier, inc=1, device_id=partner, device_id_type=MESH)
    report = jnp.where(sect == 2, 0, before)
    for to in members:
        pl.semaphore_signal(barrier, inc=1, device_id={"sect": report, "slab": to}, device_id_type=MESH)

    @pl.when(sect == half)
    def _():
        pl.semaphore_signal(barrier, inc=1, device_id={"sect": last}, device_id_type=MESH)

    @pl.when(sect == 0)
    def _():
        pl.semaphore_signal(barrier, inc=1, device_id={"sect": last, "slab": mirror}, device_id_type=MESH)

    loads = [pltpu.make_async_copy(src_hbm.at[0], src_v.at[0], load_sem.at[3])]
    loads += [
        pltpu.make_async_copy(ref.at[0], mats.at[i], load_sem.at[i])
        for i, ref in enumerate((fwd_hbm, inv_hbm, upp_hbm))
    ]
    for load in loads:
        load.start()

    def lend(ref, to, i, device):
        return pltpu.make_async_remote_copy(
            src_ref=ref.at[0], dst_ref=to, send_sem=lend_sent.at[i], recv_sem=lend_sem.at[i],
            device_id=device, device_id_type=MESH,
        )

    lends = [
        lend(fwd_hbm, mats.at[3], 0, partner),
        lend(inv_hbm, mats.at[4], 1, partner),
        lend(upp_hbm, mats.at[5], 2, partner),
        lend(src_hbm, src_v.at[1], 3, partner),
    ]
    turn_lends = [
        lend(inv_hbm, mats.at[6], 4, {"sect": half}),
        lend(inv_hbm, mats.at[6], 4, {"sect": 0, "slab": mirror}),
    ]

    def send_all(tile, gathered, sent, sem, c, to_sect, place):
        for to in members:
            pltpu.make_async_remote_copy(
                src_ref=tile.at[c], dst_ref=gathered.at[c, place],
                send_sem=sent.at[c], recv_sem=sem.at[c],
                device_id={"sect": to_sect, "slab": to}, device_id_type=MESH,
            ).start()

    def wait_for(gathered, sem, c):
        pltpu.make_async_copy(gathered.at[c], gathered.at[c], sem.at[c]).wait()

    def turn_source(p):
        both = src_v[p].astype(jnp.float32)
        turned = jnp.concatenate([both[:, :modes], both[:, modes:]], axis=0).T
        for c in range(firsts[p], firsts[p] + counts[p]):
            src_t[c] = turned[c * width:(c + 1) * width]

    def prepare(i):
        if i < 3:
            loads[1 + i].wait()
        elif i < 6:
            lends[i - 3].wait_recv()
        else:
            turn_lends[0].wait_recv()

        def pair(j, _):
            at = pl.ds(pl.multiple_of(j * 2 * rows, 2 * rows), 2 * rows)
            p0 = mats[i, 0, :, at].astype(jnp.float32).T.astype(jnp.bfloat16)
            p1 = mats[i, 1, :, at].astype(jnp.float32).T.astype(jnp.bfloat16)
            blocks = []
            for k in range(2):
                q0, q1 = p0[k * rows:(k + 1) * rows], p1[k * rows:(k + 1) * rows]
                blocks.append(jnp.concatenate([q0, q1], axis=1))
                blocks.append(jnp.concatenate([-q1, q0], axis=1))
            weights[i, pl.ds(pl.multiple_of(j * 4 * rows, 4 * rows), 4 * rows)] = jnp.concatenate(blocks, axis=0)
            return 0

        lax.fori_loop(0, slabs // 2, pair, 0)

    def apply(i, gathered, c):
        lhs = jnp.concatenate([gathered[c, k] for k in range(slabs)], axis=1)
        return jnp.dot(lhs, weights[i], preferred_element_type=jnp.float32)

    def each_chunk(p, body):
        start = p * OWN
        stop = jnp.where(p == 0, OWN, CHUNKS)

        def step(c, _):
            body(c)
            return 0
        lax.fori_loop(start, stop, step, 0)

    def run_forward(p, v):
        place = jnp.where(p == 0, slab, mirror)

        def first(c):
            f_tile[c] = src_t[c].astype(jnp.bfloat16)
            send_all(f_tile, f_all, f_sent, f_sem, c, after, place)

        def forward(c):
            wait_for(f_all, f_sem, c)
            f_tile[c] = (src_t[c] + apply(3 * p, f_all, c)).astype(jnp.bfloat16)

            @pl.when(v < last)
            def _():
                send_all(f_tile, f_all, f_sent, f_sem, c, after, place)

            @pl.when(v == last)
            def _():
                send_all(f_tile, t_all, f_sent, t_sem, c, lax.rem(sect + sections - 3, sections), place)

            pltpu.make_async_remote_copy(
                src_ref=f_all.at[c], dst_ref=s_all.at[c],
                send_sem=back_sem.at[c], recv_sem=s_sem.at[c],
                device_id={"sect": before}, device_id_type=MESH,
            ).start()

        @pl.when(v == 0)
        def _():
            each_chunk(p, first)

        @pl.when(v > 0)
        def _():
            each_chunk(p, forward)

    def run_scale(p, v):
        def scale(c):
            wait_for(s_all, s_sem, c)
            scaled[c] = apply(3 * p + 1, s_all, c)

        @pl.when(v < last)
        def _():
            each_chunk(p, scale)

    def run_turn(p):
        place = jnp.where(p == 0, slab, mirror)

        def turn(c):
            wait_for(t_all, t_sem, c)
            t_tile[c] = apply(6, t_all, c).astype(jnp.bfloat16)
            send_all(t_tile, w_all, t_sent, w_sem, c, lax.rem(sect + 2, sections), place)

        each_chunk(p, turn)

    def run_backward(p, v):
        place = jnp.where(p == 0, slab, mirror)

        def backward(c):
            wait_for(w_all, w_sem, c)
            w_tile[c] = (scaled[c] - apply(3 * p + 2, w_all, c)).astype(jnp.bfloat16)

            @pl.when(v > 0)
            def _():
                send_all(w_tile, w_all, w_sent, w_sem, c, before, place)

        @pl.when(v < last)
        def _():
            each_chunk(p, backward)

    def go_home(tile, to, first, count, i, device):
        return pltpu.make_async_remote_copy(
            src_ref=tile.at[pl.ds(first, count)], dst_ref=to,
            send_sem=home_sent.at[i], recv_sem=home_sem.at[i],
            device_id=device, device_id_type=MESH,
        )

    own_part = w_tile.at[pl.ds(0, OWN)]
    homes = [
        go_home(w_tile, w_home, OWN, CHUNKS - OWN, 0, partner),
        pltpu.make_async_remote_copy(
            src_ref=t_tile.at[pl.ds(OWN, CHUNKS - OWN)], dst_ref=w_home,
            send_sem=home_sent.at[1], recv_sem=home_sem.at[0],
            device_id={"sect": last, "slab": mirror}, device_id_type=MESH,
        ),
        go_home(t_tile, own_part, 0, OWN, 1, {"sect": last}),
    ]

    greeted = jnp.where(sect == 0, 2 * slabs + 1, jnp.where(sect == 1, 1, slabs + 1))
    greeted = jnp.where(sect == last, slabs + 3, greeted)
    pl.semaphore_wait(barrier, greeted)
    lends[3].start()
    lends[0].start()

    loads[0].wait()
    turn_source(0)

    @pl.when(sect == 0)
    def _():
        run_forward(low_pipe, low)

    @pl.when(sect == half)
    def _():
        lends[3].wait_recv()
        turn_source(1)
        run_forward(low_pipe, low)

    @pl.when(sect != half)
    def _():
        lends[3].wait_recv()
        turn_source(1)

    prepare(0)

    @pl.when(sect != 1)
    def _():
        prepare(1)
        prepare(2)
        prepare(3)

    @pl.when(low > 0)
    def _():
        run_forward(low_pipe, low)

    lends[0].wait_send()
    lends[1].start()
    lends[2].start()

    @pl.when(sect == last)
    def _():
        turn_lends[0].start()
        turn_lends[1].start()

    @pl.when(sect == 1)
    def _():
        prepare(1)
        prepare(2)
        prepare(3)

    run_forward(high_pipe, high)
    prepare(4)
    prepare(5)
    run_scale(low_pipe, low)
    run_scale(high_pipe, high)

    @pl.when(low == 0)
    def _():
        prepare(6)
        run_turn(high_pipe)

        @pl.when(sect == 0)
        def _():
            homes[1].start()

        @pl.when(sect == half)
        def _():
            homes[2].start()

    run_backward(high_pipe, high)

    @pl.when(jnp.logical_not(upper) & (sect != half - 1))
    def _():
        homes[0].start()

    run_backward(low_pipe, low)

    @pl.when(upper)
    def _():
        homes[0].start()

    @pl.when(sect == last)
    def _():
        pltpu.make_async_copy(own_part, own_part, home_sem.at[1]).wait()

    pltpu.make_async_copy(w_home, w_home, home_sem.at[0]).wait()
    wave = jnp.concatenate(
        [w_tile[c] for c in range(OWN)] + [w_home[c] for c in range(CHUNKS - OWN)], axis=0
    ).astype(jnp.float32).T
    out_ref[0] = jnp.concatenate([wave[:rows], wave[rows:]], axis=1).astype(jnp.bfloat16)

    def drain(p, v):
        def one(c):
            wait_for(f_all, f_sent, c)

            @pl.when(v > 0)
            def _():
                wait_for(f_all, back_sem, c)

            @pl.when((v > 0) & (v < last))
            def _():
                wait_for(w_all, w_sent, c)

            @pl.when(v == half)
            def _():
                wait_for(w_all, t_sent, c)

        each_chunk(p, one)

    drain(low_pipe, low)
    drain(high_pipe, high)
    for i in range(1, 4):
        lends[i].wait_send()

    @pl.when(sect == last)
    def _():
        pltpu.make_async_copy(mats.at[pl.ds(0, 2)], mats.at[pl.ds(0, 2)], lend_sent.at[4]).wait()

    @pl.when(sect != half - 1)
    def _():
        homes[0].wait_send()

    @pl.when(sect == 0)
    def _():
        pltpu.make_async_copy(w_home, w_home, home_sent.at[1]).wait()

    @pl.when(sect == half)
    def _():
        homes[2].wait_send()


def per_device(source, forward_mult, schur_inverse, upper_mult):
    sections = lax.axis_size("sect")
    slabs = lax.axis_size("slab")
    _, rows, columns = source.shape
    width = columns // 2 // CHUNKS
    gathered = pltpu.VMEM((CHUNKS, slabs, width, 2 * rows), jnp.bfloat16)
    tile = pltpu.VMEM((CHUNKS, width, 2 * rows), jnp.bfloat16)
    tile32 = pltpu.VMEM((CHUNKS, width, 2 * rows), jnp.float32)
    return pl.pallas_call(
        functools.partial(kernel, sections, slabs),
        out_shape=jax.ShapeDtypeStruct(source.shape, source.dtype),
        in_specs=[pl.BlockSpec(memory_space=pltpu.HBM)] * 4,
        out_specs=pl.BlockSpec(memory_space=pltpu.VMEM),
        scratch_shapes=[
            pltpu.VMEM((2, rows, columns), jnp.bfloat16),
            pltpu.VMEM((7, 2, rows, slabs * rows), jnp.bfloat16),
            pltpu.VMEM((7, slabs * 2 * rows, 2 * rows), jnp.bfloat16),
            tile32,
            tile32,
            tile,
            tile,
            tile,
            pltpu.VMEM((CHUNKS - OWN, width, 2 * rows), jnp.bfloat16),
            gathered,
            gathered,
            gathered,
            gathered,
            pltpu.SemaphoreType.DMA((4,)),
            pltpu.SemaphoreType.DMA((CHUNKS,)),
            pltpu.SemaphoreType.DMA((CHUNKS,)),
            pltpu.SemaphoreType.DMA((CHUNKS,)),
            pltpu.SemaphoreType.DMA((CHUNKS,)),
            pltpu.SemaphoreType.DMA((CHUNKS,)),
            pltpu.SemaphoreType.DMA((CHUNKS,)),
            pltpu.SemaphoreType.DMA((CHUNKS,)),
            pltpu.SemaphoreType.DMA((CHUNKS,)),
            pltpu.SemaphoreType.DMA((5,)),
            pltpu.SemaphoreType.DMA((5,)),
            pltpu.SemaphoreType.DMA((2,)),
            pltpu.SemaphoreType.DMA((2,)),
        ],
        compiler_params=pltpu.CompilerParams(
            collective_id=0, has_side_effects=True, vmem_limit_bytes=40 * 1024 * 1024
        ),
    )(source, forward_mult, schur_inverse, upper_mult)


def solution(mesh):
    in_specs = (
        P(("energy", "sect"), "slab", None),
        P(("energy", "sect"), None, "slab", None),
        P(("energy", "sect"), None, "slab", None),
        P(("energy", "sect"), None, "slab", None),
    )
    out_specs = P(("energy", "sect"), "slab", None)
    return jax.shard_map(
        per_device, mesh=mesh, in_specs=in_specs, out_specs=out_specs, check_vma=False
    )
```

```python
import functools

import jax
import jax.numpy as jnp
from jax import lax
from jax.experimental import pallas as pl
from jax.experimental.pallas import tpu as pltpu
from jax.sharding import PartitionSpec as P

MESH = pl.DeviceIdType.MESH
CHUNKS = 8
OWN = 5


def kernel(sections, slabs, src_hbm, fwd_hbm, inv_hbm, upp_hbm, out_ref,
           src_v, mats, weights, src_t, scaled, f_tile, w_tile, t_tile, w_home,
           f_all, s_all, w_all, t_all, load_sem, f_sent, w_sent, t_sent,
           f_sem, s_sem, w_sem, t_sem, back_sem, lend_sent, lend_sem, home_sent, home_sem):
    sect = lax.axis_index("sect")
    slab = lax.axis_index("slab")
    planes = slabs // 2
    z, y = slab // 2, lax.rem(slab, 2)
    last = sections - 1
    half = sections // 2
    rows = src_v.shape[1]
    modes = src_v.shape[2] // 2
    width = modes // CHUNKS
    mirror = slab + 1 - 2 * y
    partner = {"sect": lax.rem(sect + half, sections), "slab": mirror}
    after = lax.rem(sect + 1, sections)
    before = lax.rem(sect + last, sections)
    upper = sect >= half
    low_pipe = jnp.where(upper, 1, 0)
    high_pipe = 1 - low_pipe
    low = lax.rem(sect, half)
    high = low + half
    firsts = (0, OWN)
    counts = (OWN, CHUNKS - OWN)

    members = []
    for i in range(planes):
        reach = planes // 2 - (i + 1) // 2
        zz = lax.rem(z + (reach if i % 2 else planes - reach), planes)
        members += [zz * 2 + 1 - y, zz * 2 + y]

    barrier = pltpu.get_barrier_semaphore()
    pl.semaphore_signal(barrier, inc=1, device_id=partner, device_id_type=MESH)
    report = jnp.where(sect == 2, 0, before)
    for to in members:
        pl.semaphore_signal(barrier, inc=1, device_id={"sect": report, "slab": to}, device_id_type=MESH)

    @pl.when(sect == half)
    def _():
        pl.semaphore_signal(barrier, inc=1, device_id={"sect": last}, device_id_type=MESH)

    @pl.when(sect == 0)
    def _():
        pl.semaphore_signal(barrier, inc=1, device_id={"sect": last, "slab": mirror}, device_id_type=MESH)

    loads = [pltpu.make_async_copy(src_hbm.at[0], src_v.at[0], load_sem.at[3])]
    loads += [
        pltpu.make_async_copy(ref.at[0], mats.at[i], load_sem.at[i])
        for i, ref in enumerate((fwd_hbm, inv_hbm, upp_hbm))
    ]
    for load in loads:
        load.start()

    def lend(ref, to, i, device):
        return pltpu.make_async_remote_copy(
            src_ref=ref.at[0], dst_ref=to, send_sem=lend_sent.at[i], recv_sem=lend_sem.at[i],
            device_id=device, device_id_type=MESH,
        )

    lends = [
        lend(fwd_hbm, mats.at[3], 0, partner),
        lend(inv_hbm, mats.at[4], 1, partner),
        lend(upp_hbm, mats.at[5], 2, partner),
        lend(src_hbm, src_v.at[1], 3, partner),
    ]
    turn_lends = [
        lend(inv_hbm, mats.at[6], 4, {"sect": half}),
        lend(inv_hbm, mats.at[6], 4, {"sect": 0, "slab": mirror}),
    ]

    def send_all(tile, gathered, sent, sem, c, to_sect, place):
        for to in members:
            pltpu.make_async_remote_copy(
                src_ref=tile.at[c], dst_ref=gathered.at[c, place],
                send_sem=sent.at[c], recv_sem=sem.at[c],
                device_id={"sect": to_sect, "slab": to}, device_id_type=MESH,
            ).start()

    def wait_for(gathered, sem, c):
        pltpu.make_async_copy(gathered.at[c], gathered.at[c], sem.at[c]).wait()

    def turn_source(p):
        both = src_v[p].astype(jnp.float32)
        turned = jnp.concatenate([both[:, :modes], both[:, modes:]], axis=0).T
        for c in range(firsts[p], firsts[p] + counts[p]):
            src_t[c] = turned[c * width:(c + 1) * width]

    def prepare(i):
        if i < 3:
            loads[1 + i].wait()
        elif i < 6:
            lends[i - 3].wait_recv()
        else:
            turn_lends[0].wait_recv()

        def pair(j, _):
            at = pl.ds(pl.multiple_of(j * 2 * rows, 2 * rows), 2 * rows)
            p0 = mats[i, 0, :, at].astype(jnp.float32).T.astype(jnp.bfloat16)
            p1 = mats[i, 1, :, at].astype(jnp.float32).T.astype(jnp.bfloat16)
            blocks = []
            for k in range(2):
                q0, q1 = p0[k * rows:(k + 1) * rows], p1[k * rows:(k + 1) * rows]
                blocks.append(jnp.concatenate([q0, q1], axis=1))
                blocks.append(jnp.concatenate([-q1, q0], axis=1))
            weights[i, pl.ds(pl.multiple_of(j * 4 * rows, 4 * rows), 4 * rows)] = jnp.concatenate(blocks, axis=0)
            return 0

        lax.fori_loop(0, slabs // 2, pair, 0)

    def apply(i, gathered, c):
        lhs = jnp.concatenate([gathered[c, k] for k in range(slabs)], axis=1)
        return jnp.dot(lhs, weights[i], preferred_element_type=jnp.float32)

    def each_chunk(p, body):
        start = p * OWN
        stop = jnp.where(p == 0, OWN, CHUNKS)

        def step(c, _):
            body(c)
            return 0
        lax.fori_loop(start, stop, step, 0)

    def run_forward(p, v):
        place = jnp.where(p == 0, slab, mirror)

        def first(c):
            f_tile[c] = src_t[c].astype(jnp.bfloat16)
            send_all(f_tile, f_all, f_sent, f_sem, c, after, place)

        def forward(c):
            wait_for(f_all, f_sem, c)
            f_tile[c] = (src_t[c] + apply(3 * p, f_all, c)).astype(jnp.bfloat16)

            @pl.when(v < last)
            def _():
                send_all(f_tile, f_all, f_sent, f_sem, c, after, place)

            @pl.when(v == last)
            def _():
                send_all(f_tile, t_all, f_sent, t_sem, c, lax.rem(sect + sections - 3, sections), place)

        def hand_back(c):
            pltpu.make_async_remote_copy(
                src_ref=f_all.at[c], dst_ref=s_all.at[c],
                send_sem=back_sem.at[c], recv_sem=s_sem.at[c],
                device_id={"sect": before}, device_id_type=MESH,
            ).start()

        @pl.when(v == 0)
        def _():
            each_chunk(p, first)

        @pl.when(v > 0)
        def _():
            each_chunk(p, forward)
            each_chunk(p, hand_back)

    def run_scale(p, v):
        def scale(c):
            wait_for(s_all, s_sem, c)
            scaled[c] = apply(3 * p + 1, s_all, c)

        @pl.when(v < last)
        def _():
            each_chunk(p, scale)

    def run_turn(p):
        place = jnp.where(p == 0, slab, mirror)

        def turn(c):
            wait_for(t_all, t_sem, c)
            t_tile[c] = apply(6, t_all, c).astype(jnp.bfloat16)
            send_all(t_tile, w_all, t_sent, w_sem, c, lax.rem(sect + 2, sections), place)

        each_chunk(p, turn)

    def run_backward(p, v):
        place = jnp.where(p == 0, slab, mirror)

        def backward(c):
            wait_for(w_all, w_sem, c)
            w_tile[c] = (scaled[c] - apply(3 * p + 2, w_all, c)).astype(jnp.bfloat16)

            @pl.when(v > 0)
            def _():
                send_all(w_tile, w_all, w_sent, w_sem, c, before, place)

        @pl.when(v < last)
        def _():
            each_chunk(p, backward)

    def go_home(tile, to, first, count, i, device):
        return pltpu.make_async_remote_copy(
            src_ref=tile.at[pl.ds(first, count)], dst_ref=to,
            send_sem=home_sent.at[i], recv_sem=home_sem.at[i],
            device_id=device, device_id_type=MESH,
        )

    own_part = w_tile.at[pl.ds(0, OWN)]
    homes = [
        go_home(w_tile, w_home, OWN, CHUNKS - OWN, 0, partner),
        pltpu.make_async_remote_copy(
            src_ref=t_tile.at[pl.ds(OWN, CHUNKS - OWN)], dst_ref=w_home,
            send_sem=home_sent.at[1], recv_sem=home_sem.at[0],
            device_id={"sect": last, "slab": mirror}, device_id_type=MESH,
        ),
        go_home(t_tile, own_part, 0, OWN, 1, {"sect": last}),
    ]

    loads[0].wait()
    turn_source(0)
    greeted = jnp.where(sect == 0, 2 * slabs + 1, jnp.where(sect == 1, 1, slabs + 1))
    greeted = jnp.where(sect == last, slabs + 3, greeted)
    pl.semaphore_wait(barrier, greeted)
    lends[3].start()

    @pl.when(sect == 0)
    def _():
        run_forward(low_pipe, low)

    @pl.when(sect > 0)
    def _():
        lends[0].start()

    @pl.when(sect == last)
    def _():
        turn_lends[0].start()
        turn_lends[1].start()

    @pl.when(sect == half)
    def _():
        lends[3].wait_recv()
        turn_source(1)
        run_forward(low_pipe, low)

    @pl.when(sect != half)
    def _():
        lends[3].wait_recv()
        turn_source(1)

    prepare(0)

    @pl.when(sect != 1)
    def _():
        prepare(1)
        prepare(2)

        @pl.when(sect != half)
        def _():
            prepare(3)

    @pl.when(low > 0)
    def _():
        run_forward(low_pipe, low)

    @pl.when(sect > 0)
    def _():
        lends[0].wait_send()

    @pl.when((sect != half - 1) & (sect != last))
    def _():
        lends[1].start()
        lends[2].start()

    @pl.when(sect == 1)
    def _():
        prepare(1)
        prepare(2)
        prepare(3)

    run_forward(high_pipe, high)

    @pl.when(sect == half - 1)
    def _():
        lends[1].start()
        lends[2].start()

    @pl.when(sect != half - 1)
    def _():
        prepare(4)
        prepare(5)

    run_scale(low_pipe, low)
    run_scale(high_pipe, high)

    @pl.when(low == 0)
    def _():
        prepare(6)
        run_turn(high_pipe)

        @pl.when(sect == 0)
        def _():
            homes[1].start()

        @pl.when(sect == half)
        def _():
            homes[2].start()

    run_backward(high_pipe, high)

    @pl.when(jnp.logical_not(upper) & (sect != half - 1))
    def _():
        homes[0].start()

    run_backward(low_pipe, low)

    @pl.when(upper)
    def _():
        homes[0].start()

    @pl.when(sect == last)
    def _():
        pltpu.make_async_copy(own_part, own_part, home_sem.at[1]).wait()

    pltpu.make_async_copy(w_home, w_home, home_sem.at[0]).wait()
    wave = jnp.concatenate(
        [w_tile[c] for c in range(OWN)] + [w_home[c] for c in range(CHUNKS - OWN)], axis=0
    ).astype(jnp.float32).T
    out_ref[0] = jnp.concatenate([wave[:rows], wave[rows:]], axis=1).astype(jnp.bfloat16)

    def drain(p, v):
        def one(c):
            wait_for(f_all, f_sent, c)

            @pl.when(v > 0)
            def _():
                wait_for(f_all, back_sem, c)

            @pl.when((v > 0) & (v < last))
            def _():
                wait_for(w_all, w_sent, c)

            @pl.when(v == half)
            def _():
                wait_for(w_all, t_sent, c)

        each_chunk(p, one)

    drain(low_pipe, low)
    drain(high_pipe, high)
    lends[3].wait_send()

    @pl.when(sect < last)
    def _():
        lends[1].wait_send()
        lends[2].wait_send()

    @pl.when(sect == last)
    def _():
        pltpu.make_async_copy(mats.at[pl.ds(0, 2)], mats.at[pl.ds(0, 2)], lend_sent.at[4]).wait()

    @pl.when(sect != half - 1)
    def _():
        homes[0].wait_send()

    @pl.when(sect == 0)
    def _():
        pltpu.make_async_copy(w_home, w_home, home_sent.at[1]).wait()

    @pl.when(sect == half)
    def _():
        homes[2].wait_send()


def per_device(source, forward_mult, schur_inverse, upper_mult):
    sections = lax.axis_size("sect")
    slabs = lax.axis_size("slab")
    _, rows, columns = source.shape
    width = columns // 2 // CHUNKS
    gathered = pltpu.VMEM((CHUNKS, slabs, width, 2 * rows), jnp.bfloat16)
    tile = pltpu.VMEM((CHUNKS, width, 2 * rows), jnp.bfloat16)
    tile32 = pltpu.VMEM((CHUNKS, width, 2 * rows), jnp.float32)
    return pl.pallas_call(
        functools.partial(kernel, sections, slabs),
        out_shape=jax.ShapeDtypeStruct(source.shape, source.dtype),
        in_specs=[pl.BlockSpec(memory_space=pltpu.HBM)] * 4,
        out_specs=pl.BlockSpec(memory_space=pltpu.VMEM),
        scratch_shapes=[
            pltpu.VMEM((2, rows, columns), jnp.bfloat16),
            pltpu.VMEM((7, 2, rows, slabs * rows), jnp.bfloat16),
            pltpu.VMEM((7, slabs * 2 * rows, 2 * rows), jnp.bfloat16),
            tile32,
            tile32,
            tile,
            tile,
            tile,
            pltpu.VMEM((CHUNKS - OWN, width, 2 * rows), jnp.bfloat16),
            gathered,
            gathered,
            gathered,
            gathered,
            pltpu.SemaphoreType.DMA((4,)),
            pltpu.SemaphoreType.DMA((CHUNKS,)),
            pltpu.SemaphoreType.DMA((CHUNKS,)),
            pltpu.SemaphoreType.DMA((CHUNKS,)),
            pltpu.SemaphoreType.DMA((CHUNKS,)),
            pltpu.SemaphoreType.DMA((CHUNKS,)),
            pltpu.SemaphoreType.DMA((CHUNKS,)),
            pltpu.SemaphoreType.DMA((CHUNKS,)),
            pltpu.SemaphoreType.DMA((CHUNKS,)),
            pltpu.SemaphoreType.DMA((5,)),
            pltpu.SemaphoreType.DMA((5,)),
            pltpu.SemaphoreType.DMA((2,)),
            pltpu.SemaphoreType.DMA((2,)),
        ],
        compiler_params=pltpu.CompilerParams(
            collective_id=0, has_side_effects=True, vmem_limit_bytes=40 * 1024 * 1024
        ),
    )(source, forward_mult, schur_inverse, upper_mult)


def solution(mesh):
    in_specs = (
        P(("energy", "sect"), "slab", None),
        P(("energy", "sect"), None, "slab", None),
        P(("energy", "sect"), None, "slab", None),
        P(("energy", "sect"), None, "slab", None),
    )
    out_specs = P(("energy", "sect"), "slab", None)
    return jax.shard_map(
        per_device, mesh=mesh, in_specs=in_specs, out_specs=out_specs, check_vma=False
    )
```

```python
import functools

import jax
import jax.numpy as jnp
from jax import lax
from jax.experimental import pallas as pl
from jax.experimental.pallas import tpu as pltpu
from jax.sharding import PartitionSpec as P

MESH = pl.DeviceIdType.MESH
CHUNKS = 8
OWN = 5


def kernel(sections, slabs, src_hbm, fwd_hbm, inv_hbm, upp_hbm, out_ref,
           src_v, mats, weights, src_t, scaled, f_tile, w_tile, t_tile, w_home,
           f_all, s_all, w_all, t_all, load_sem, f_sent, w_sent, t_sent,
           f_sem, s_sem, w_sem, t_sem, back_sem, lend_sent, lend_sem, home_sent, home_sem):
    sect = lax.axis_index("sect")
    slab = lax.axis_index("slab")
    planes = slabs // 2
    z, y = slab // 2, lax.rem(slab, 2)
    last = sections - 1
    half = sections // 2
    rows = src_v.shape[1]
    modes = src_v.shape[2] // 2
    width = modes // CHUNKS
    mirror = slab + 1 - 2 * y
    partner = {"sect": lax.rem(sect + half, sections), "slab": mirror}
    after = lax.rem(sect + 1, sections)
    before = lax.rem(sect + last, sections)
    upper = sect >= half
    low_pipe = jnp.where(upper, 1, 0)
    high_pipe = 1 - low_pipe
    low = lax.rem(sect, half)
    high = low + half
    firsts = (0, OWN)
    counts = (OWN, CHUNKS - OWN)

    members, order = [], []
    far = sum(planes // 2 - (i + 1) // 2 > 3 * planes // 8 for i in range(planes))
    for i in range(planes):
        reach = planes // 2 - (i + 1) // 2
        zz = lax.rem(z + (reach if i % 2 else planes - reach), planes)
        order.append(zz)
        members += [zz * 2 + 1 - y, zz * 2 + y]

    barrier = pltpu.get_barrier_semaphore()
    pl.semaphore_signal(barrier, inc=1, device_id=partner, device_id_type=MESH)
    report = jnp.where(sect == 2, 0, before)
    for to in members:
        pl.semaphore_signal(barrier, inc=1, device_id={"sect": report, "slab": to}, device_id_type=MESH)

    @pl.when(sect == half)
    def _():
        pl.semaphore_signal(barrier, inc=1, device_id={"sect": last}, device_id_type=MESH)

    @pl.when(sect == 0)
    def _():
        pl.semaphore_signal(barrier, inc=1, device_id={"sect": last, "slab": mirror}, device_id_type=MESH)

    loads = [pltpu.make_async_copy(src_hbm.at[0], src_v.at[0], load_sem.at[3])]
    loads += [
        pltpu.make_async_copy(ref.at[0], mats.at[i], load_sem.at[i])
        for i, ref in enumerate((fwd_hbm, inv_hbm, upp_hbm))
    ]
    for load in loads:
        load.start()

    def lend(ref, to, i, device):
        return pltpu.make_async_remote_copy(
            src_ref=ref.at[0], dst_ref=to, send_sem=lend_sent.at[i], recv_sem=lend_sem.at[i],
            device_id=device, device_id_type=MESH,
        )

    lends = [
        lend(fwd_hbm, mats.at[3], 0, partner),
        lend(inv_hbm, mats.at[4], 1, partner),
        lend(upp_hbm, mats.at[5], 2, partner),
        lend(src_hbm, src_v.at[1], 3, partner),
    ]
    turn_lends = [
        lend(inv_hbm, mats.at[6], 4, {"sect": half}),
        lend(inv_hbm, mats.at[6], 4, {"sect": 0, "slab": mirror}),
    ]

    def send_all(tile, gathered, sent, sem, c, to_sect, place):
        for n, to in enumerate(members):
            pltpu.make_async_remote_copy(
                src_ref=tile.at[c], dst_ref=gathered.at[c, place],
                send_sem=sent.at[c], recv_sem=sem.at[c if n < 2 * far else CHUNKS + c],
                device_id={"sect": to_sect, "slab": to}, device_id_type=MESH,
            ).start()

    def wait_for(gathered, sem, c):
        pltpu.make_async_copy(gathered.at[c], gathered.at[c], sem.at[c]).wait()

    def turn_source(p):
        both = src_v[p].astype(jnp.float32)
        turned = jnp.concatenate([both[:, :modes], both[:, modes:]], axis=0).T
        for c in range(firsts[p], firsts[p] + counts[p]):
            src_t[c] = turned[c * width:(c + 1) * width]

    def prepare(i):
        if i < 3:
            loads[1 + i].wait()
        elif i < 6:
            lends[i - 3].wait_recv()
        else:
            turn_lends[0].wait_recv()

        def pair(j, _):
            at = pl.ds(pl.multiple_of(j * 2 * rows, 2 * rows), 2 * rows)
            p0 = mats[i, 0, :, at].astype(jnp.float32).T.astype(jnp.bfloat16)
            p1 = mats[i, 1, :, at].astype(jnp.float32).T.astype(jnp.bfloat16)
            blocks = []
            for k in range(2):
                q0, q1 = p0[k * rows:(k + 1) * rows], p1[k * rows:(k + 1) * rows]
                blocks.append(jnp.concatenate([q0, q1], axis=1))
                blocks.append(jnp.concatenate([-q1, q0], axis=1))
            weights[i, pl.ds(pl.multiple_of(j * 4 * rows, 4 * rows), 4 * rows)] = jnp.concatenate(blocks, axis=0)
            return 0

        lax.fori_loop(0, slabs // 2, pair, 0)

    def apply(i, gathered, c):
        lhs = jnp.concatenate([gathered[c, k] for k in range(slabs)], axis=1)
        return jnp.dot(lhs, weights[i], preferred_element_type=jnp.float32)

    def arriving(i, gathered, sem, c):
        total = None
        for first, group in ((CHUNKS, order[far:]), (0, order[:far])):
            if not group:
                continue
            part = gathered.at[c, pl.ds(0, 2 * len(group))]
            pltpu.make_async_copy(part, part, sem.at[first + c]).wait()
            for zz in group:
                lhs = jnp.concatenate([gathered[c, 2 * zz], gathered[c, 2 * zz + 1]], axis=1)
                rhs = weights[i, pl.ds(pl.multiple_of(zz * 4 * rows, 4 * rows), 4 * rows)]
                term = jnp.dot(lhs, rhs, preferred_element_type=jnp.float32)
                total = term if total is None else total + term
        return total

    def each_chunk(p, body):
        start = p * OWN
        stop = jnp.where(p == 0, OWN, CHUNKS)

        def step(c, _):
            body(c)
            return 0
        lax.fori_loop(start, stop, step, 0)

    def run_forward(p, v):
        place = jnp.where(p == 0, slab, mirror)

        def first(c):
            f_tile[c] = src_t[c].astype(jnp.bfloat16)
            send_all(f_tile, f_all, f_sent, f_sem, c, after, place)

        def forward(c):
            f_tile[c] = (src_t[c] + arriving(3 * p, f_all, f_sem, c)).astype(jnp.bfloat16)

            @pl.when(v < last)
            def _():
                send_all(f_tile, f_all, f_sent, f_sem, c, after, place)

            @pl.when(v == last)
            def _():
                send_all(f_tile, t_all, f_sent, t_sem, c, lax.rem(sect + sections - 3, sections), place)

        def hand_back(c):
            pltpu.make_async_remote_copy(
                src_ref=f_all.at[c], dst_ref=s_all.at[c],
                send_sem=back_sem.at[c], recv_sem=s_sem.at[c],
                device_id={"sect": before}, device_id_type=MESH,
            ).start()

        @pl.when(v == 0)
        def _():
            each_chunk(p, first)

        @pl.when(v > 0)
        def _():
            each_chunk(p, forward)
            each_chunk(p, hand_back)

    def run_scale(p, v):
        def scale(c):
            wait_for(s_all, s_sem, c)
            scaled[c] = apply(3 * p + 1, s_all, c)

        @pl.when(v < last)
        def _():
            each_chunk(p, scale)

    def run_turn(p):
        place = jnp.where(p == 0, slab, mirror)

        def turn(c):
            t_tile[c] = arriving(6, t_all, t_sem, c).astype(jnp.bfloat16)
            send_all(t_tile, w_all, t_sent, w_sem, c, lax.rem(sect + 2, sections), place)

        each_chunk(p, turn)

    def run_backward(p, v):
        place = jnp.where(p == 0, slab, mirror)

        def backward(c):
            w_tile[c] = (scaled[c] - arriving(3 * p + 2, w_all, w_sem, c)).astype(jnp.bfloat16)

            @pl.when(v > 0)
            def _():
                send_all(w_tile, w_all, w_sent, w_sem, c, before, place)

        @pl.when(v < last)
        def _():
            each_chunk(p, backward)

    def go_home(tile, to, first, count, i, device):
        return pltpu.make_async_remote_copy(
            src_ref=tile.at[pl.ds(first, count)], dst_ref=to,
            send_sem=home_sent.at[i], recv_sem=home_sem.at[i],
            device_id=device, device_id_type=MESH,
        )

    own_part = w_tile.at[pl.ds(0, OWN)]
    homes = [
        go_home(w_tile, w_home, OWN, CHUNKS - OWN, 0, partner),
        pltpu.make_async_remote_copy(
            src_ref=t_tile.at[pl.ds(OWN, CHUNKS - OWN)], dst_ref=w_home,
            send_sem=home_sent.at[1], recv_sem=home_sem.at[0],
            device_id={"sect": last, "slab": mirror}, device_id_type=MESH,
        ),
        go_home(t_tile, own_part, 0, OWN, 1, {"sect": last}),
    ]

    loads[0].wait()
    turn_source(0)
    greeted = jnp.where(sect == 0, 2 * slabs + 1, jnp.where(sect == 1, 1, slabs + 1))
    greeted = jnp.where(sect == last, slabs + 3, greeted)
    pl.semaphore_wait(barrier, greeted)
    lends[3].start()

    @pl.when(sect == 0)
    def _():
        run_forward(low_pipe, low)

    @pl.when(sect > 0)
    def _():
        lends[0].start()

    @pl.when(sect == last)
    def _():
        turn_lends[0].start()
        turn_lends[1].start()

    @pl.when(sect == half)
    def _():
        lends[3].wait_recv()
        turn_source(1)
        run_forward(low_pipe, low)

    @pl.when(sect != half)
    def _():
        lends[3].wait_recv()
        turn_source(1)

    prepare(0)

    @pl.when(sect != 1)
    def _():
        prepare(1)
        prepare(2)

        @pl.when(sect != half)
        def _():
            prepare(3)

    @pl.when(low > 0)
    def _():
        run_forward(low_pipe, low)

    @pl.when(sect > 0)
    def _():
        lends[0].wait_send()

    @pl.when((sect != half - 1) & (sect != last))
    def _():
        lends[1].start()
        lends[2].start()

    @pl.when(sect == 1)
    def _():
        prepare(1)
        prepare(2)
        prepare(3)

    run_forward(high_pipe, high)

    @pl.when(sect == half - 1)
    def _():
        lends[1].start()
        lends[2].start()

    @pl.when(sect != half - 1)
    def _():
        prepare(4)
        prepare(5)

    run_scale(low_pipe, low)
    run_scale(high_pipe, high)

    @pl.when(low == 0)
    def _():
        prepare(6)
        run_turn(high_pipe)

        @pl.when(sect == 0)
        def _():
            homes[1].start()

        @pl.when(sect == half)
        def _():
            homes[2].start()

    run_backward(high_pipe, high)

    @pl.when(jnp.logical_not(upper) & (sect != half - 1))
    def _():
        homes[0].start()

    run_backward(low_pipe, low)

    @pl.when(upper)
    def _():
        homes[0].start()

    @pl.when(sect == last)
    def _():
        pltpu.make_async_copy(own_part, own_part, home_sem.at[1]).wait()

    pltpu.make_async_copy(w_home, w_home, home_sem.at[0]).wait()
    wave = jnp.concatenate(
        [w_tile[c] for c in range(OWN)] + [w_home[c] for c in range(CHUNKS - OWN)], axis=0
    ).astype(jnp.float32).T
    out_ref[0] = jnp.concatenate([wave[:rows], wave[rows:]], axis=1).astype(jnp.bfloat16)

    def drain(p, v):
        def one(c):
            wait_for(f_all, f_sent, c)

            @pl.when(v > 0)
            def _():
                wait_for(f_all, back_sem, c)

            @pl.when((v > 0) & (v < last))
            def _():
                wait_for(w_all, w_sent, c)

            @pl.when(v == half)
            def _():
                wait_for(w_all, t_sent, c)

        each_chunk(p, one)

    drain(low_pipe, low)
    drain(high_pipe, high)
    lends[3].wait_send()

    @pl.when(sect < last)
    def _():
        lends[1].wait_send()
        lends[2].wait_send()

    @pl.when(sect == last)
    def _():
        pltpu.make_async_copy(mats.at[pl.ds(0, 2)], mats.at[pl.ds(0, 2)], lend_sent.at[4]).wait()

    @pl.when(sect != half - 1)
    def _():
        homes[0].wait_send()

    @pl.when(sect == 0)
    def _():
        pltpu.make_async_copy(w_home, w_home, home_sent.at[1]).wait()

    @pl.when(sect == half)
    def _():
        homes[2].wait_send()


def per_device(source, forward_mult, schur_inverse, upper_mult):
    sections = lax.axis_size("sect")
    slabs = lax.axis_size("slab")
    _, rows, columns = source.shape
    width = columns // 2 // CHUNKS
    gathered = pltpu.VMEM((CHUNKS, slabs, width, 2 * rows), jnp.bfloat16)
    tile = pltpu.VMEM((CHUNKS, width, 2 * rows), jnp.bfloat16)
    tile32 = pltpu.VMEM((CHUNKS, width, 2 * rows), jnp.float32)
    return pl.pallas_call(
        functools.partial(kernel, sections, slabs),
        out_shape=jax.ShapeDtypeStruct(source.shape, source.dtype),
        in_specs=[pl.BlockSpec(memory_space=pltpu.HBM)] * 4,
        out_specs=pl.BlockSpec(memory_space=pltpu.VMEM),
        scratch_shapes=[
            pltpu.VMEM((2, rows, columns), jnp.bfloat16),
            pltpu.VMEM((7, 2, rows, slabs * rows), jnp.bfloat16),
            pltpu.VMEM((7, slabs * 2 * rows, 2 * rows), jnp.bfloat16),
            tile32,
            tile32,
            tile,
            tile,
            tile,
            pltpu.VMEM((CHUNKS - OWN, width, 2 * rows), jnp.bfloat16),
            gathered,
            gathered,
            gathered,
            gathered,
            pltpu.SemaphoreType.DMA((4,)),
            pltpu.SemaphoreType.DMA((2 * CHUNKS,)),
            pltpu.SemaphoreType.DMA((2 * CHUNKS,)),
            pltpu.SemaphoreType.DMA((2 * CHUNKS,)),
            pltpu.SemaphoreType.DMA((2 * CHUNKS,)),
            pltpu.SemaphoreType.DMA((2 * CHUNKS,)),
            pltpu.SemaphoreType.DMA((2 * CHUNKS,)),
            pltpu.SemaphoreType.DMA((2 * CHUNKS,)),
            pltpu.SemaphoreType.DMA((2 * CHUNKS,)),
            pltpu.SemaphoreType.DMA((5,)),
            pltpu.SemaphoreType.DMA((5,)),
            pltpu.SemaphoreType.DMA((2,)),
            pltpu.SemaphoreType.DMA((2,)),
        ],
        compiler_params=pltpu.CompilerParams(
            collective_id=0, has_side_effects=True, vmem_limit_bytes=40 * 1024 * 1024
        ),
    )(source, forward_mult, schur_inverse, upper_mult)


def solution(mesh):
    in_specs = (
        P(("energy", "sect"), "slab", None),
        P(("energy", "sect"), None, "slab", None),
        P(("energy", "sect"), None, "slab", None),
        P(("energy", "sect"), None, "slab", None),
    )
    out_specs = P(("energy", "sect"), "slab", None)
    return jax.shard_map(
        per_device, mesh=mesh, in_specs=in_specs, out_specs=out_specs, check_vma=False
    )
```

```python
import functools

import jax
import jax.numpy as jnp
from jax import lax
from jax.experimental import pallas as pl
from jax.experimental.pallas import tpu as pltpu
from jax.sharding import PartitionSpec as P

MESH = pl.DeviceIdType.MESH
CHUNKS = 8
OWN = 5


def kernel(sections, slabs, src_hbm, fwd_hbm, inv_hbm, upp_hbm, out_ref,
           src_v, mats, weights, src_t, scaled, f_tile, w_tile, t_tile, w_home,
           f_all, s_all, w_all, t_all, load_sem, f_sent, w_sent, t_sent,
           f_sem, s_sem, w_sem, t_sem, back_sem, lend_sent, lend_sem, home_sent, home_sem):
    sect = lax.axis_index("sect")
    slab = lax.axis_index("slab")
    planes = slabs // 2
    z, y = slab // 2, lax.rem(slab, 2)
    last = sections - 1
    half = sections // 2
    rows = src_v.shape[1]
    modes = src_v.shape[2] // 2
    width = modes // CHUNKS
    mirror = slab + 1 - 2 * y
    partner = {"sect": lax.rem(sect + half, sections), "slab": mirror}
    after = lax.rem(sect + 1, sections)
    before = lax.rem(sect + last, sections)
    upper = sect >= half
    low_pipe = jnp.where(upper, 1, 0)
    high_pipe = 1 - low_pipe
    low = lax.rem(sect, half)
    high = low + half
    firsts = (0, OWN)
    counts = (OWN, CHUNKS - OWN)

    members, order = [], []
    far = sum(planes // 2 - (i + 1) // 2 > 7 * planes // 16 for i in range(planes))
    for i in range(planes):
        reach = planes // 2 - (i + 1) // 2
        zz = lax.rem(z + (reach if i % 2 else planes - reach), planes)
        order.append(zz)
        members += [zz * 2 + 1 - y, zz * 2 + y]

    barrier = pltpu.get_barrier_semaphore()
    pl.semaphore_signal(barrier, inc=1, device_id=partner, device_id_type=MESH)
    report = jnp.where(sect == 2, 0, before)
    for to in members:
        pl.semaphore_signal(barrier, inc=1, device_id={"sect": report, "slab": to}, device_id_type=MESH)

    @pl.when(sect == half)
    def _():
        pl.semaphore_signal(barrier, inc=1, device_id={"sect": last}, device_id_type=MESH)

    @pl.when(sect == 0)
    def _():
        pl.semaphore_signal(barrier, inc=1, device_id={"sect": last, "slab": mirror}, device_id_type=MESH)

    loads = [pltpu.make_async_copy(src_hbm.at[0], src_v.at[0], load_sem.at[3])]
    loads += [
        pltpu.make_async_copy(ref.at[0], mats.at[i], load_sem.at[i])
        for i, ref in enumerate((fwd_hbm, inv_hbm, upp_hbm))
    ]
    for load in loads:
        load.start()

    def lend(ref, to, i, device):
        return pltpu.make_async_remote_copy(
            src_ref=ref.at[0], dst_ref=to, send_sem=lend_sent.at[i], recv_sem=lend_sem.at[i],
            device_id=device, device_id_type=MESH,
        )

    lends = [
        lend(fwd_hbm, mats.at[3], 0, partner),
        lend(inv_hbm, mats.at[4], 1, partner),
        lend(upp_hbm, mats.at[5], 2, partner),
        lend(src_hbm, src_v.at[1], 3, partner),
    ]
    turn_lends = [
        lend(inv_hbm, mats.at[6], 4, {"sect": half}),
        lend(inv_hbm, mats.at[6], 4, {"sect": 0, "slab": mirror}),
    ]

    def send_all(tile, gathered, sent, sem, c, to_sect, place):
        for n, to in enumerate(members):
            pltpu.make_async_remote_copy(
                src_ref=tile.at[c], dst_ref=gathered.at[c, place],
                send_sem=sent.at[c], recv_sem=sem.at[c if n < 2 * far else CHUNKS + c],
                device_id={"sect": to_sect, "slab": to}, device_id_type=MESH,
            ).start()

    def wait_for(gathered, sem, c):
        pltpu.make_async_copy(gathered.at[c], gathered.at[c], sem.at[c]).wait()

    def turn_source(p):
        both = src_v[p].astype(jnp.float32)
        turned = jnp.concatenate([both[:, :modes], both[:, modes:]], axis=0).T
        for c in range(firsts[p], firsts[p] + counts[p]):
            src_t[c] = turned[c * width:(c + 1) * width]

    def prepare(i):
        if i < 3:
            loads[1 + i].wait()
        elif i < 6:
            lends[i - 3].wait_recv()
        else:
            turn_lends[0].wait_recv()

        def pair(j, _):
            at = pl.ds(pl.multiple_of(j * 2 * rows, 2 * rows), 2 * rows)
            p0 = mats[i, 0, :, at].astype(jnp.float32).T.astype(jnp.bfloat16)
            p1 = mats[i, 1, :, at].astype(jnp.float32).T.astype(jnp.bfloat16)
            blocks = []
            for k in range(2):
                q0, q1 = p0[k * rows:(k + 1) * rows], p1[k * rows:(k + 1) * rows]
                blocks.append(jnp.concatenate([q0, q1], axis=1))
                blocks.append(jnp.concatenate([-q1, q0], axis=1))
            weights[i, pl.ds(pl.multiple_of(j * 4 * rows, 4 * rows), 4 * rows)] = jnp.concatenate(blocks, axis=0)
            return 0

        lax.fori_loop(0, slabs // 2, pair, 0)

    def apply(i, gathered, c):
        lhs = jnp.concatenate([gathered[c, k] for k in range(slabs)], axis=1)
        return jnp.dot(lhs, weights[i], preferred_element_type=jnp.float32)

    def arriving(i, gathered, sem, c):
        total = None
        for first, group in ((CHUNKS, order[far:]), (0, order[:far])):
            if not group:
                continue
            part = gathered.at[c, pl.ds(0, 2 * len(group))]
            pltpu.make_async_copy(part, part, sem.at[first + c]).wait()
            for zz in group:
                lhs = jnp.concatenate([gathered[c, 2 * zz], gathered[c, 2 * zz + 1]], axis=1)
                rhs = weights[i, pl.ds(pl.multiple_of(zz * 4 * rows, 4 * rows), 4 * rows)]
                term = jnp.dot(lhs, rhs, preferred_element_type=jnp.float32)
                total = term if total is None else total + term
        return total

    def each_chunk(p, body):
        start = p * OWN
        stop = jnp.where(p == 0, OWN, CHUNKS)

        def step(c, _):
            body(c)
            return 0
        lax.fori_loop(start, stop, step, 0)

    def run_forward(p, v):
        place = jnp.where(p == 0, slab, mirror)

        def first(c):
            f_tile[c] = src_t[c].astype(jnp.bfloat16)
            send_all(f_tile, f_all, f_sent, f_sem, c, after, place)

        def forward(c):
            f_tile[c] = (src_t[c] + arriving(3 * p, f_all, f_sem, c)).astype(jnp.bfloat16)

            @pl.when(v < last)
            def _():
                send_all(f_tile, f_all, f_sent, f_sem, c, after, place)

            @pl.when(v == last)
            def _():
                send_all(f_tile, t_all, f_sent, t_sem, c, lax.rem(sect + sections - 3, sections), place)

        def hand_back(c):
            pltpu.make_async_remote_copy(
                src_ref=f_all.at[c], dst_ref=s_all.at[c],
                send_sem=back_sem.at[c], recv_sem=s_sem.at[c],
                device_id={"sect": before}, device_id_type=MESH,
            ).start()

        @pl.when(v == 0)
        def _():
            each_chunk(p, first)

        @pl.when(v > 0)
        def _():
            each_chunk(p, forward)
            each_chunk(p, hand_back)

    def run_scale(p, v):
        def scale(c):
            wait_for(s_all, s_sem, c)
            scaled[c] = apply(3 * p + 1, s_all, c)

        @pl.when(v < last)
        def _():
            each_chunk(p, scale)

    def run_turn(p):
        place = jnp.where(p == 0, slab, mirror)

        def turn(c):
            t_tile[c] = arriving(6, t_all, t_sem, c).astype(jnp.bfloat16)
            send_all(t_tile, w_all, t_sent, w_sem, c, lax.rem(sect + 2, sections), place)

        each_chunk(p, turn)

    def run_backward(p, v):
        place = jnp.where(p == 0, slab, mirror)

        def backward(c):
            w_tile[c] = (scaled[c] - arriving(3 * p + 2, w_all, w_sem, c)).astype(jnp.bfloat16)

            @pl.when(v > 0)
            def _():
                send_all(w_tile, w_all, w_sent, w_sem, c, before, place)

        @pl.when(v < last)
        def _():
            each_chunk(p, backward)

    def go_home(tile, to, first, count, i, device):
        return pltpu.make_async_remote_copy(
            src_ref=tile.at[pl.ds(first, count)], dst_ref=to,
            send_sem=home_sent.at[i], recv_sem=home_sem.at[i],
            device_id=device, device_id_type=MESH,
        )

    own_part = w_tile.at[pl.ds(0, OWN)]
    homes = [
        go_home(w_tile, w_home, OWN, CHUNKS - OWN, 0, partner),
        pltpu.make_async_remote_copy(
            src_ref=t_tile.at[pl.ds(OWN, CHUNKS - OWN)], dst_ref=w_home,
            send_sem=home_sent.at[1], recv_sem=home_sem.at[0],
            device_id={"sect": last, "slab": mirror}, device_id_type=MESH,
        ),
        go_home(t_tile, own_part, 0, OWN, 1, {"sect": last}),
    ]

    loads[0].wait()
    turn_source(0)
    greeted = jnp.where(sect == 0, 2 * slabs + 1, jnp.where(sect == 1, 1, slabs + 1))
    greeted = jnp.where(sect == last, slabs + 3, greeted)
    pl.semaphore_wait(barrier, greeted)
    lends[3].start()

    @pl.when(sect == 0)
    def _():
        run_forward(low_pipe, low)

    @pl.when(sect > 0)
    def _():
        lends[0].start()

    @pl.when(sect == last)
    def _():
        turn_lends[0].start()
        turn_lends[1].start()

    @pl.when(sect == half)
    def _():
        lends[3].wait_recv()
        turn_source(1)
        run_forward(low_pipe, low)

    @pl.when(sect != half)
    def _():
        lends[3].wait_recv()
        turn_source(1)

    prepare(0)

    @pl.when(sect != 1)
    def _():
        prepare(1)
        prepare(2)

        @pl.when(sect != half)
        def _():
            prepare(3)

    @pl.when(low > 0)
    def _():
        run_forward(low_pipe, low)

    @pl.when(sect > 0)
    def _():
        lends[0].wait_send()

    @pl.when((sect != half - 1) & (sect != last))
    def _():
        lends[1].start()
        lends[2].start()

    @pl.when(sect == 1)
    def _():
        prepare(1)
        prepare(2)
        prepare(3)

    run_forward(high_pipe, high)

    @pl.when(sect == half - 1)
    def _():
        lends[1].start()
        lends[2].start()

    @pl.when(sect != half - 1)
    def _():
        prepare(4)
        prepare(5)

    run_scale(low_pipe, low)
    run_scale(high_pipe, high)

    @pl.when(low == 0)
    def _():
        prepare(6)
        run_turn(high_pipe)

        @pl.when(sect == 0)
        def _():
            homes[1].start()

        @pl.when(sect == half)
        def _():
            homes[2].start()

    run_backward(high_pipe, high)

    @pl.when(jnp.logical_not(upper) & (sect != half - 1))
    def _():
        homes[0].start()

    run_backward(low_pipe, low)

    @pl.when(upper)
    def _():
        homes[0].start()

    @pl.when(sect == last)
    def _():
        pltpu.make_async_copy(own_part, own_part, home_sem.at[1]).wait()

    pltpu.make_async_copy(w_home, w_home, home_sem.at[0]).wait()
    wave = jnp.concatenate(
        [w_tile[c] for c in range(OWN)] + [w_home[c] for c in range(CHUNKS - OWN)], axis=0
    ).astype(jnp.float32).T
    out_ref[0] = jnp.concatenate([wave[:rows], wave[rows:]], axis=1).astype(jnp.bfloat16)

    def drain(p, v):
        def one(c):
            wait_for(f_all, f_sent, c)

            @pl.when(v > 0)
            def _():
                wait_for(f_all, back_sem, c)

            @pl.when((v > 0) & (v < last))
            def _():
                wait_for(w_all, w_sent, c)

            @pl.when(v == half)
            def _():
                wait_for(w_all, t_sent, c)

        each_chunk(p, one)

    drain(low_pipe, low)
    drain(high_pipe, high)
    lends[3].wait_send()

    @pl.when(sect < last)
    def _():
        lends[1].wait_send()
        lends[2].wait_send()

    @pl.when(sect == last)
    def _():
        pltpu.make_async_copy(mats.at[pl.ds(0, 2)], mats.at[pl.ds(0, 2)], lend_sent.at[4]).wait()

    @pl.when(sect != half - 1)
    def _():
        homes[0].wait_send()

    @pl.when(sect == 0)
    def _():
        pltpu.make_async_copy(w_home, w_home, home_sent.at[1]).wait()

    @pl.when(sect == half)
    def _():
        homes[2].wait_send()


def per_device(source, forward_mult, schur_inverse, upper_mult):
    sections = lax.axis_size("sect")
    slabs = lax.axis_size("slab")
    _, rows, columns = source.shape
    width = columns // 2 // CHUNKS
    gathered = pltpu.VMEM((CHUNKS, slabs, width, 2 * rows), jnp.bfloat16)
    tile = pltpu.VMEM((CHUNKS, width, 2 * rows), jnp.bfloat16)
    tile32 = pltpu.VMEM((CHUNKS, width, 2 * rows), jnp.float32)
    return pl.pallas_call(
        functools.partial(kernel, sections, slabs),
        out_shape=jax.ShapeDtypeStruct(source.shape, source.dtype),
        in_specs=[pl.BlockSpec(memory_space=pltpu.HBM)] * 4,
        out_specs=pl.BlockSpec(memory_space=pltpu.VMEM),
        scratch_shapes=[
            pltpu.VMEM((2, rows, columns), jnp.bfloat16),
            pltpu.VMEM((7, 2, rows, slabs * rows), jnp.bfloat16),
            pltpu.VMEM((7, slabs * 2 * rows, 2 * rows), jnp.bfloat16),
            tile32,
            tile32,
            tile,
            tile,
            tile,
            pltpu.VMEM((CHUNKS - OWN, width, 2 * rows), jnp.bfloat16),
            gathered,
            gathered,
            gathered,
            gathered,
            pltpu.SemaphoreType.DMA((4,)),
            pltpu.SemaphoreType.DMA((2 * CHUNKS,)),
            pltpu.SemaphoreType.DMA((2 * CHUNKS,)),
            pltpu.SemaphoreType.DMA((2 * CHUNKS,)),
            pltpu.SemaphoreType.DMA((2 * CHUNKS,)),
            pltpu.SemaphoreType.DMA((2 * CHUNKS,)),
            pltpu.SemaphoreType.DMA((2 * CHUNKS,)),
            pltpu.SemaphoreType.DMA((2 * CHUNKS,)),
            pltpu.SemaphoreType.DMA((2 * CHUNKS,)),
            pltpu.SemaphoreType.DMA((5,)),
            pltpu.SemaphoreType.DMA((5,)),
            pltpu.SemaphoreType.DMA((2,)),
            pltpu.SemaphoreType.DMA((2,)),
        ],
        compiler_params=pltpu.CompilerParams(
            collective_id=0, has_side_effects=True, vmem_limit_bytes=40 * 1024 * 1024
        ),
    )(source, forward_mult, schur_inverse, upper_mult)


def solution(mesh):
    in_specs = (
        P(("energy", "sect"), "slab", None),
        P(("energy", "sect"), None, "slab", None),
        P(("energy", "sect"), None, "slab", None),
        P(("energy", "sect"), None, "slab", None),
    )
    out_specs = P(("energy", "sect"), "slab", None)
    return jax.shard_map(
        per_device, mesh=mesh, in_specs=in_specs, out_specs=out_specs, check_vma=False
    )
```
